32 devices in a mesh: rep: 16 (over z, y, x), shard: 2 (over core).
Axes of the slice: x: 2, y: 2, z: 4, core: 2. Of those that a mesh axis runs over, the one named last changes fastest.
Arguments:
- images: bfloat16 [192, 196, 512], P(('rep', 'shard')), may hold values from -6 to 6
- cotangent: bfloat16 [192, 196, 512], P(('rep', 'shard')), may hold values from -6 to 6
- window_map: int32 [2, 196], replicated, may hold values from 0 to 195, as said below
- shift_mask: int32 [4, 49, 49], replicated, may hold values from 0 to 1, as said below
- rel_index: int32 [49, 49], replicated, may hold values from 0 to 168, as said below
- attend_weight: float32 [2, 512, 1536], P(None, 'shard'), may hold values from -0.25 to 0.25
- attend_moment: float32 [2, 512, 1536], P(None, 'shard'), may hold values from -128 to 128
- attend_square: float32 [2, 512, 1536], P(None, 'shard'), may hold values from 37.632 to 150.528
- output_weight: float32 [2, 512, 512], P(None, 'shard'), may hold values from -0.75 to 0.75
- output_moment: float32 [2, 512, 512], P(None, 'shard'), may hold values from -40 to 40
- output_square: float32 [2, 512, 512], P(None, 'shard'), may hold values from 3.38688 to 13.54752
- expand_weight: float32 [2, 512, 2048], P(None, 'shard'), may hold values from -0.25 to 0.25
- expand_moment: float32 [2, 512, 2048], P(None, 'shard'), may hold values from -40 to 40
- expand_square: float32 [2, 512, 2048], P(None, 'shard'), may hold values from 3.38688 to 13.54752
- reduce_weight: float32 [2, 2048, 512], P(None, 'shard'), may hold values from -0.125 to 0.125
- reduce_moment: float32 [2, 2048, 512], P(None, 'shard'), may hold values from -80 to 80
- reduce_square: float32 [2, 2048, 512], P(None, 'shard'), may hold values from 13.54752 to 54.19008
- bias_table: float32 [2, 16, 169], P(None, 'shard'), may hold values from -6 to 6
- table_moment: float32 [2, 16, 169], P(None, 'shard'), may hold values from -112 to 112
- table_square: float32 [2, 16, 169], P(None, 'shard'), may hold values from 27.09504 to 109.1328
- layer_vectors: float32 [2, 6, 512], P(None, None, 'shard')
- vector_moment: float32 [2, 6, 512], P(None, None, 'shard'), may hold values from -128 to 128
- vector_square: float32 [2, 6, 512], P(None, None, 'shard'), may hold values from 37.632 to 150.528
- wide_bias: float32 [2, 3072], P(None, 'shard'), may hold values from -3 to 3
- biases_moment: float32 [2, 3072], P(None, 'shard'), may hold values from -80 to 80
- biases_square: float32 [2, 3072], P(None, 'shard'), may hold values from 13.54752 to 54.19008
Outputs:
- block_out: bfloat16 [192, 196, 512], P(('rep', 'shard'))
- input_grad: float32 [192, 196, 512], P(('rep', 'shard'))
- moment_attend: float32 [2, 512, 1536], P(None, 'shard')
- square_attend: float32 [2, 512, 1536], P(None, 'shard')
- updated_attend: float32 [2, 512, 1536], P(None, 'shard')
- moment_output: float32 [2, 512, 512], P(None, 'shard')
- square_output: float32 [2, 512, 512], P(None, 'shard')
- updated_output: float32 [2, 512, 512], P(None, 'shard')
- moment_expand: float32 [2, 512, 2048], P(None, 'shard')
- square_expand: float32 [2, 512, 2048], P(None, 'shard')
- updated_expand: float32 [2, 512, 2048], P(None, 'shard')
- moment_reduce: float32 [2, 2048, 512], P(None, 'shard')
- square_reduce: float32 [2, 2048, 512], P(None, 'shard')
- updated_reduce: float32 [2, 2048, 512], P(None, 'shard')
- moment_table: float32 [2, 16, 169], P(None, 'shard')
- square_table: float32 [2, 16, 169], P(None, 'shard')
- updated_table: float32 [2, 16, 169], P(None, 'shard')
- moment_vectors: float32 [2, 6, 512], P(None, None, 'shard')
- square_vectors: float32 [2, 6, 512], P(None, None, 'shard')
- updated_vectors: float32 [2, 6, 512], P(None, None, 'shard')
- moment_biases: float32 [2, 3072], P(None, 'shard')
- square_biases: float32 [2, 3072], P(None, 'shard')
- updated_biases: float32 [2, 3072], P(None, 'shard')
The draws below stay inside these ranges and needn't reach their ends.
Inputs may be any that keep to these rules, and one draw needn't show every extreme that they name: `window_map`: each row is a permutation of the 196 tokens, slots listed window by window; within a window slot j sits at the same grid place in every window, and odd rows are even rows cyclically shifted on the 14 x 14 grid. `shift_mask`: 1 where two slots of a window lie in different regions of the shifted grid. `rel_index`: pairs of slots with equal grid offset share a row, different offsets take different rows.
All inputs are finite; a program needn't handle non-finite values.
Results may differ from the reference program's by a relative error of at most 0.028.
Values may be sent and summed in bfloat16 or wider, within the bound.
A program may use at most 320 MiB of HBM per device.

```python
import math
import jax
import jax.numpy as jnp
from jax import lax

D = 512
HEADS = 16
FF = 2048
WIN = 7
SIDE = 14
LAYERS = 2
STEP = 10
IMG_DEV = 6
TOK = 196
WTOK = 49
WINS = 4
RELS = 169
IMAGES = 192
TOKENS = 37632
N_SHARD = 2


def geometry(key):
    slots = jax.random.permutation(jax.random.fold_in(key, 11), WTOK).astype(jnp.int32)
    shifts = jax.random.randint(jax.random.fold_in(key, 12), (2,), 1, WIN).astype(jnp.int32)
    labels = jax.random.permutation(jax.random.fold_in(key, 13), RELS).astype(jnp.int32)
    return (slots, shifts, labels)


def slot_places(slots):
    slot_ids = jnp.arange(TOK, dtype=jnp.int32)
    window = slot_ids // WTOK
    inner = slots[slot_ids % WTOK]
    across = SIDE // WIN
    row = window // across * WIN + inner // WIN
    column = window % across * WIN + inner % WIN
    return (row, column)


def draw_window_map(key, part):
    slots, shifts, labels = geometry(key)
    row, column = slot_places(slots)
    maps = []
    for layer in range(LAYERS):
        odd = layer % 2
        moved_row = (row + odd * shifts[0]) % SIDE
        moved_column = (column + odd * shifts[1]) % SIDE
        maps.append(moved_row * SIDE + moved_column)
    return jnp.stack(maps).astype(jnp.int32)


def draw_shift_mask(key, part):
    slots, shifts, labels = geometry(key)
    row, column = slot_places(slots)
    region_row = jnp.where(row < SIDE - WIN, 0, jnp.where(row < SIDE - shifts[0], 1, 2))
    region_column = jnp.where(column < SIDE - WIN, 0, jnp.where(column < SIDE - shifts[1], 1, 2))
    region = (region_row * 3 + region_column).reshape(WINS, WTOK)
    return (region[:, :, None] != region[:, None, :]).astype(jnp.int32)


def draw_rel_index(key, part):
    slots, shifts, labels = geometry(key)
    row = slots // WIN
    column = slots % WIN
    offset = (row[:, None] - row[None, :] + WIN - 1) * (2 * WIN - 1) + (column[:, None] - column[None, :] + WIN - 1)
    return labels[offset].astype(jnp.int32)


def draw_layer_vectors(key, part):
    key = jax.random.fold_in(key, 5)
    noise = jax.random.normal(key, (LAYERS, 6, D), jnp.float32)
    kind = jnp.array([1.0, 0.0, 0.0, 1.0, 0.0, 0.0], jnp.float32)[None, :, None]
    return kind * (1.0 + 0.1 * noise) + (1.0 - kind) * 0.3 * noise


def levels(own_key, shape, cuts, smallest, high):
    def one(dim, parts):
        steps = jax.random.uniform(jax.random.fold_in(jax.random.fold_in(own_key, 6), dim), (parts,), jnp.float32, smallest / len(cuts), high / len(cuts))
        return jnp.repeat(jnp.exp(steps), shape[dim] // parts).reshape((-1,) + (1,) * (len(shape) - dim - 1))

    factor_of = one(*cuts[0])
    for cut in cuts[1:]:
        factor_of = factor_of * one(*cut)
    return factor_of


def normal_values(own_key, dims, scale, limit, shards=(), kind=jnp.bfloat16):
    values = jax.random.normal(own_key, dims, jnp.float32) * scale
    if len(shards) > 0:
        values = levels(own_key, dims, shards, -0.22, 0.18) * values
    return jnp.clip(values, min=-limit, max=limit).astype(kind)


def setup_inputs(seed: int = 0) -> dict:
    arg_keys = jax.random.split(jax.random.key(seed), 27)
    return {
        "images": normal_values(arg_keys[0], (IMAGES, TOK, D), 1.0, 6.0, ((0, 32),)),
        "cotangent": normal_values(arg_keys[1], (IMAGES, TOK, D), 1.0, 6.0, ((0, 32),)),
        "window_map": draw_window_map(jax.random.fold_in(arg_keys[26], 71), 0),
        "shift_mask": draw_shift_mask(jax.random.fold_in(arg_keys[26], 71), 0),
        "rel_index": draw_rel_index(jax.random.fold_in(arg_keys[26], 71), 0),
        "attend_weight": normal_values(arg_keys[5], (LAYERS, D, 3 * D), D ** -0.5, 0.25, ((1, 2),), jnp.float32),
        "attend_moment": normal_values(arg_keys[6], (LAYERS, D, 3 * D), (0.11 * TOKENS ** 0.5), 128.0, ((1, 2),), jnp.float32),
        "attend_square": jnp.clip(jnp.exp(math.log(150.528) - 1.3862944 * jax.random.uniform(arg_keys[7], (LAYERS, D, 3 * D), jnp.float32) ** levels(arg_keys[7], (LAYERS, D, 3 * D), ((1, 2),), -0.2, 0.2)), 37.632, 150.528),
        "output_weight": normal_values(arg_keys[8], (LAYERS, D, D), (D // 8) ** -0.5, 0.75, ((1, 2),), jnp.float32),
        "output_moment": normal_values(arg_keys[9], (LAYERS, D, D), (0.033 * TOKENS ** 0.5), 40.0, ((1, 2),), jnp.float32),
        "output_square": jnp.clip(jnp.exp(math.log(13.54752) - 1.3862944 * jax.random.uniform(arg_keys[10], (LAYERS, D, D), jnp.float32) ** levels(arg_keys[10], (LAYERS, D, D), ((1, 2),), -0.2, 0.2)), 3.38688, 13.54752),
        "expand_weight": normal_values(arg_keys[11], (LAYERS, D, FF), D ** -0.5, 0.25, ((1, 2),), jnp.float32),
        "expand_moment": normal_values(arg_keys[12], (LAYERS, D, FF), (0.033 * TOKENS ** 0.5), 40.0, ((1, 2),), jnp.float32),
        "expand_square": jnp.clip(jnp.exp(math.log(13.54752) - 1.3862944 * jax.random.uniform(arg_keys[13], (LAYERS, D, FF), jnp.float32) ** levels(arg_keys[13], (LAYERS, D, FF), ((1, 2),), -0.2, 0.2)), 3.38688, 13.54752),
        "reduce_weight": normal_values(arg_keys[14], (LAYERS, FF, D), FF ** -0.5, 0.125, ((1, 2),), jnp.float32),
        "reduce_moment": normal_values(arg_keys[15], (LAYERS, FF, D), (0.066 * TOKENS ** 0.5), 80.0, ((1, 2),), jnp.float32),
        "reduce_square": jnp.clip(jnp.exp(math.log(54.19008) - 1.3862944 * jax.random.uniform(arg_keys[16], (LAYERS, FF, D), jnp.float32) ** levels(arg_keys[16], (LAYERS, FF, D), ((1, 2),), -0.2, 0.2)), 13.54752, 54.19008),
        "bias_table": normal_values(arg_keys[17], (LAYERS, HEADS, RELS), 1.0, 6.0, ((1, 2),), jnp.float32),
        "table_moment": normal_values(arg_keys[18], (LAYERS, HEADS, RELS), (0.094 * TOKENS ** 0.5), 112.0, ((1, 2),), jnp.float32),
        "table_square": jnp.clip(jnp.exp(math.log(109.1328) - 1.3932148 * jax.random.uniform(arg_keys[19], (LAYERS, HEADS, RELS), jnp.float32) ** levels(arg_keys[19], (LAYERS, HEADS, RELS), ((1, 2),), -0.2, 0.2)), 27.09504, 109.1328),
        "layer_vectors": draw_layer_vectors(jax.random.fold_in(arg_keys[26], 71), 0),
        "vector_moment": normal_values(arg_keys[21], (LAYERS, 6, D), (0.11 * TOKENS ** 0.5), 128.0, ((2, 2),), jnp.float32),
        "vector_square": jnp.clip(jnp.exp(math.log(150.528) - 1.3862944 * jax.random.uniform(arg_keys[22], (LAYERS, 6, D), jnp.float32) ** levels(arg_keys[22], (LAYERS, 6, D), ((2, 2),), -0.2, 0.2)), 37.632, 150.528),
        "wide_bias": normal_values(arg_keys[23], (LAYERS, 2 * D + FF), 0.5, 3.0, ((1, 2),), jnp.float32),
        "biases_moment": normal_values(arg_keys[24], (LAYERS, 2 * D + FF), (0.066 * TOKENS ** 0.5), 80.0, ((1, 2),), jnp.float32),
        "biases_square": jnp.clip(jnp.exp(math.log(54.19008) - 1.3862944 * jax.random.uniform(arg_keys[25], (LAYERS, 2 * D + FF), jnp.float32) ** levels(arg_keys[25], (LAYERS, 2 * D + FF), ((1, 2),), -0.2, 0.2)), 13.54752, 54.19008),
    }


@jax.custom_vjp
def low(v):
    return lax.optimization_barrier(v.astype(jnp.bfloat16)).astype(jnp.float32)

@jax.custom_vjp
def low_back(v):
    return v

def low_keep(v):
    return (low(v), None)

def low_pass(kept, grad):
    return (grad,)

def back_keep(v):
    return (v, None)

def back_low(kept, grad):
    return (low(grad),)
low.defvjp(low_keep, low_pass)
low_back.defvjp(back_keep, back_low)
HIGH = lax.Precision.HIGHEST

def norm_rows(v, gain, shift):
    mean = lax.optimization_barrier(jnp.mean(v, axis=-1, keepdims=True))
    centered = v - mean
    var = lax.optimization_barrier(jnp.mean(centered * centered, axis=-1, keepdims=True))
    return centered * lax.rsqrt(var + 1e-05) * gain + shift

def gelu_exact(v):
    return 0.5 * v * (1.0 + jax.scipy.special.erf(v * 0.7071067811865476))

def block(state, order, penalty, rel_index, attend, output, expand, shrink, table, gains, offsets):
    width = attend.shape[0]
    count = state.shape[0]
    tokens = state.shape[1]
    windows = penalty.shape[0]
    heads = table.shape[0]
    depth = width // heads
    slots_in = state[:, order, :]
    normed = low(norm_rows(slots_in, gains[0], gains[1]))
    qkv_bias = jnp.concatenate([offsets[:width], jnp.zeros((width,), jnp.float32), offsets[width:2 * width]])
    lifted = jnp.einsum('bti,in->btn', normed, attend, precision=HIGH) + qkv_bias
    lifted = low(low_back(lifted)).reshape(count, windows, tokens // windows, 3, heads, depth)
    query = lifted[:, :, :, 0]
    keys = lifted[:, :, :, 1]
    values = lifted[:, :, :, 2]
    scores = jnp.einsum('bwihc,bwjhc->bwhij', query, keys, precision=HIGH) * depth ** (-0.5)
    scores = scores + table[:, rel_index][None, None] + penalty[None, :, None]
    scores = low_back(scores)
    top = lax.optimization_barrier(jnp.max(scores, axis=-1, keepdims=True))
    expo = jnp.exp(scores - top)
    probs = low(expo / lax.optimization_barrier(jnp.sum(expo, axis=-1, keepdims=True)))
    mixed = jnp.einsum('bwhij,bwjhc->bwihc', probs, values, precision=HIGH).reshape(count, tokens, width)
    mixed = low(low_back(mixed))
    branch = low_back(jnp.einsum('bti,in->btn', mixed, output, precision=HIGH) + gains[2])
    middle = slots_in + branch
    normed_two = low(norm_rows(middle, gains[3], gains[4]))
    hidden = low_back(jnp.einsum('bti,in->btn', normed_two, expand, precision=HIGH) + offsets[2 * width:])
    activated = low(gelu_exact(hidden))
    slots_out = middle + low_back(jnp.einsum('bti,in->btn', activated, shrink, precision=HIGH) + gains[5])
    return jnp.zeros_like(state).at[:, order, :].set(slots_out)

def adam(weight, moment, square, grad, rate, decay):
    moment_new = 0.9 * moment + 0.1 * grad
    square_new = 0.999 * square + 0.001 * grad * grad
    first_hat = moment_new / (1.0 - 0.9 ** STEP)
    second_hat = square_new / (1.0 - 0.999 ** STEP)
    weight_new = weight - rate * (first_hat / (jnp.sqrt(second_hat) + 1e-08) + decay * weight)
    return (moment_new, square_new, weight_new)

def reference(images, cotangent, window_map, shift_mask, rel_index, attend_weight, attend_moment, attend_square, output_weight, output_moment, output_square, expand_weight, expand_moment, expand_square, reduce_weight, reduce_moment, reduce_square, bias_table, table_moment, table_square, layer_vectors, vector_moment, vector_square, wide_bias, biases_moment, biases_square):
    masters = (attend_weight, output_weight, expand_weight, reduce_weight, bias_table, layer_vectors, wide_bias)
    group = IMG_DEV * N_SHARD
    blocks = IMAGES // group
    source = images.astype(jnp.float32).reshape(blocks, group, TOK, D)
    incoming = cotangent.astype(jnp.float32).reshape(blocks, group, TOK, D)
    mask_term = -100.0 * shift_mask.astype(jnp.float32)

    def run(params, source):
        rounded = tuple((low(item) for item in params))

        def layers_of(state):
            for layer in range(LAYERS):
                state = block(state, window_map[layer], mask_term * float(layer % 2), rel_index, *(item[layer] for item in rounded))
            return state
        checked = jax.checkpoint(layers_of)

        def scan_step(carry, piece):
            return (carry, checked(piece))
        _, result = lax.scan(scan_step, jnp.float32(0.0), source)
        return result
    result, pullback = jax.vjp(run, masters, source)
    grads, grad_source = pullback(incoming)
    block_out = result.reshape(IMAGES, TOK, D).astype(jnp.bfloat16)
    input_grad = grad_source.reshape(IMAGES, TOK, D)
    ma, sa, wa = adam(attend_weight, attend_moment, attend_square, grads[0], 3.0 * D ** (-0.5), 0.05)
    mo, so, wo = adam(output_weight, output_moment, output_square, grads[1], 3.0 * (8.0 / D) ** 0.5, 0.05)
    me, se, we = adam(expand_weight, expand_moment, expand_square, grads[2], 3.0 * D ** (-0.5), 0.05)
    mr, sr, wr = adam(reduce_weight, reduce_moment, reduce_square, grads[3], 3.0 * FF ** (-0.5), 0.05)
    mt, st, wt = adam(bias_table, table_moment, table_square, grads[4], 3.0, 0.0)
    mv, sv, wv = adam(layer_vectors, vector_moment, vector_square, grads[5], 1.0, 0.0)
    mb, sb, wb = adam(wide_bias, biases_moment, biases_square, grads[6], 1.5, 0.0)
    return (block_out, input_grad, ma, sa, wa, mo, so, wo, me, se, we, mr, sr, wr, mt, st, wt, mv, sv, wv, mb, sb, wb)
```

```python
import jax
import jax.numpy as jnp
from jax import lax
from jax.experimental import pallas as pl
from jax.experimental.pallas import tpu as pltpu
from jax.sharding import PartitionSpec as P

D = 512
FF = 2048
STEP = 10
DEPTH = 32
LANES = 128
PACK = LANES // DEPTH
ROWS = 112
SCALE = DEPTH ** (-0.5)
BF = jnp.bfloat16
F32 = jnp.float32


def dot(left, right, dims):
    return lax.dot_general(left, right, (dims, ((), ())), preferred_element_type=F32)


def mm(left, right):
    return dot(left, right, ((1,), (0,)))


def mm_t(left, right):
    return dot(left, right, ((1,), (1,)))


def t_mm(left, right):
    return dot(left, right, ((0,), (0,)))


def head_masks():
    lane = lax.broadcasted_iota(jnp.int32, (1, LANES), 1)
    return [(lane // DEPTH == h) for h in range(PACK)]


def stack_heads(x, masks):
    return jnp.concatenate([x * m.astype(F32).astype(BF) for m in masks], axis=0)


def pad_keys(x):
    return jnp.concatenate([x, jnp.zeros((LANES - ROWS, LANES), x.dtype)], axis=0)


def pick_heads(x, masks):
    out = x[0:ROWS]
    for h in range(1, PACK):
        out = jnp.where(masks[h], x[h * ROWS : (h + 1) * ROWS], out)
    return out


def softmax_rows(s):
    e = jnp.exp(s - jnp.max(s, axis=-1, keepdims=True))
    return e * (1.0 / jnp.sum(e, axis=-1, keepdims=True))


def attend_fwd_kernel(c_ref, bias_ref, a_ref):
    masks = head_masks()
    width = a_ref.shape[1]
    for g in range(width // LANES):
        col = g * LANES
        q = c_ref[:, col : col + LANES]
        k = pad_keys(c_ref[:, width + col : width + col + LANES])
        v = pad_keys(c_ref[:, 2 * width + col : 2 * width + col + LANES])
        s = mm_t(stack_heads(q, masks), k) * SCALE
        s = s + bias_ref[0, g * PACK * ROWS : (g + 1) * PACK * ROWS, :]
        p = softmax_rows(s).astype(BF)
        a_ref[:, col : col + LANES] = pick_heads(mm(p, v), masks).astype(BF)


def attend_bwd_kernel(c_ref, da_ref, bias_ref, dc_ref, z_ref):
    masks = head_masks()
    width = da_ref.shape[1]

    @pl.when((pl.program_id(0) == 0) & (pl.program_id(1) == 0))
    def _():
        z_ref[...] = jnp.zeros_like(z_ref)

    for g in range(width // LANES):
        col = g * LANES
        rows = slice(g * PACK * ROWS, (g + 1) * PACK * ROWS)
        q = c_ref[:, col : col + LANES]
        k = pad_keys(c_ref[:, width + col : width + col + LANES])
        v = pad_keys(c_ref[:, 2 * width + col : 2 * width + col + LANES])
        qs = stack_heads(q, masks)
        ds = stack_heads(da_ref[:, col : col + LANES], masks)
        p = softmax_rows(mm_t(qs, k) * SCALE + bias_ref[0, rows, :])
        dp = mm_t(ds, v)
        inner = jnp.sum(p * dp, axis=-1, keepdims=True)
        dz = (p * (dp - inner)).astype(BF)
        z_ref[rows, :] += dz.astype(F32)
        dv = t_mm(p.astype(BF), ds)
        dk = t_mm(dz, qs) * SCALE
        dq = pick_heads(mm(dz, k), masks) * SCALE
        dc_ref[:, col : col + LANES] = dq.astype(BF)
        dc_ref[:, width + col : width + col + LANES] = dk[:ROWS].astype(BF)
        dc_ref[:, 2 * width + col : 2 * width + col + LANES] = dv[:ROWS].astype(BF)


def attend_fwd(c, bias):
    pairs, stacked, _ = bias.shape
    images = c.shape[0] // (pairs * ROWS)
    width = c.shape[1] // 3
    row = lambda t, b: (b * pairs + t, 0)
    return pl.pallas_call(
        attend_fwd_kernel,
        grid=(pairs, images),
        in_specs=[
            pl.BlockSpec((ROWS, 3 * width), row),
            pl.BlockSpec((1, stacked, LANES), lambda t, b: (t, 0, 0)),
        ],
        out_specs=pl.BlockSpec((ROWS, width), row),
        out_shape=jax.ShapeDtypeStruct((c.shape[0], width), BF),
        compiler_params=pltpu.CompilerParams(vmem_limit_bytes=32 * 1024 * 1024),
        cost_estimate=pl.CostEstimate(
            flops=4 * pairs * images * stacked * LANES * LANES,
            bytes_accessed=c.size * 3 + bias.size * 4,
            transcendentals=pairs * images * stacked * LANES,
        ),
    )(c, bias)


def attend_bwd(c, da, bias):
    pairs, stacked, _ = bias.shape
    images = c.shape[0] // (pairs * ROWS)
    width = c.shape[1] // 3
    row = lambda t, b: (b * pairs + t, 0)
    return pl.pallas_call(
        attend_bwd_kernel,
        grid=(pairs, images),
        in_specs=[
            pl.BlockSpec((ROWS, 3 * width), row),
            pl.BlockSpec((ROWS, width), row),
            pl.BlockSpec((1, stacked, LANES), lambda t, b: (t, 0, 0)),
        ],
        out_specs=[
            pl.BlockSpec((ROWS, 3 * width), row),
            pl.BlockSpec((stacked, LANES), lambda t, b: (0, 0)),
        ],
        out_shape=[
            jax.ShapeDtypeStruct(c.shape, BF),
            jax.ShapeDtypeStruct((stacked, LANES), F32),
        ],
        compiler_params=pltpu.CompilerParams(vmem_limit_bytes=32 * 1024 * 1024),
        cost_estimate=pl.CostEstimate(
            flops=10 * pairs * images * stacked * LANES * LANES,
            bytes_accessed=c.size * 5 + bias.size * 4,
            transcendentals=pairs * images * stacked * LANES,
        ),
    )(c, da, bias)


def row_stats(v):
    mean = jnp.mean(v, axis=-1, keepdims=True)
    centered = v - mean
    rstd = lax.rsqrt(jnp.mean(centered * centered, axis=-1, keepdims=True) + 1e-05)
    return mean, rstd


def norm_rows(v, gain, shift):
    mean, rstd = row_stats(v)
    return ((v - mean) * rstd * gain + shift).astype(BF), (mean, rstd)


def norm_back(v, stats, gain, do):
    mean, rstd = stats
    r = (v - mean) * rstd
    dg = do * gain
    grad = (
        dg - jnp.mean(dg, axis=-1, keepdims=True) - r * jnp.mean(dg * r, axis=-1, keepdims=True)
    ) * rstd
    return grad, jnp.sum(do * r, axis=0), jnp.sum(do, axis=0)


def gelu_both(f):
    cdf = 0.5 * (1.0 + lax.erf(f * 0.7071067811865476))
    slope = cdf + f * jnp.exp(-0.5 * f * f) * 0.3989422804014327
    return (f * cdf).astype(BF), slope.astype(BF)


def relative_table(rel_index, rows):
    return (rel_index[:, :, None] == jnp.arange(rows, dtype=jnp.int32)[None, None, :]).astype(F32)


def pair_bias(table, onehot, penalty):
    position = jnp.einsum("hr,ijr->hij", table.astype(F32), onehot, precision=lax.Precision.HIGHEST)
    size = position.shape[-1]
    both = position[None, None] + penalty.reshape(-1, 2, 1, size, size)
    first = jnp.pad(
        both[:, 0], ((0, 0), (0, 0), (0, ROWS - size), (0, LANES - size)), constant_values=-1e30
    )
    second = jnp.pad(
        both[:, 1],
        ((0, 0), (0, 0), (size, ROWS - 2 * size), (size, LANES - 2 * size)),
        constant_values=-1e30,
    )
    row = lax.broadcasted_iota(jnp.int32, (ROWS, LANES), 0)
    lane = lax.broadcasted_iota(jnp.int32, (ROWS, LANES), 1)
    both = jnp.maximum(first, second)
    both = jnp.where((row >= 2 * size) & (lane < size), 0.0, both)
    return both.reshape(penalty.shape[0] // 2, -1, LANES)


def padded_order(order, windows):
    pairs = order.reshape(windows // 2, -1)
    return jnp.pad(pairs, ((0, 0), (0, ROWS - pairs.shape[1])), constant_values=-1).reshape(-1)


def place(onehot, x, contract):
    count = x.shape[0]
    hot = jnp.broadcast_to(onehot[None], (count,) + onehot.shape)
    return lax.dot_general(
        hot, x, (((contract + 1,), (1,)), ((0,), (0,))), preferred_element_type=F32
    )


def forward_layer(s, bias, weights):
    attend, output, expand, shrink, gains, offsets = weights
    width = attend.shape[0]
    qkv_bias = jnp.concatenate(
        [offsets[:width], jnp.zeros((width,), F32), offsets[width : 2 * width]]
    )
    wide = s.astype(F32)
    u, stats_one = norm_rows(wide, gains[0], gains[1])
    c = (mm(u, attend) + qkv_bias).astype(BF)
    a = attend_fwd(c, bias)
    m = wide + mm(a, output) + gains[2]
    n, stats_two = norm_rows(m, gains[3], gains[4])
    e, slope = gelu_both(mm(n, expand) + offsets[2 * width :])
    out = (m + mm(e, shrink) + gains[5]).astype(BF)
    return out, (s, u, stats_one, c, a, m, n, stats_two, e, slope)


def backward_layer(gs, bias, weights, saved, send):
    attend, output, expand, shrink, gains, offsets = weights
    s, u, stats_one, c, a, m, n, stats_two, e, slope = saved
    dy = gs.astype(BF)
    wide = gs.astype(F32)
    grad_last = jnp.sum(dy.astype(F32), axis=0)
    grad_shrink = t_mm(e, dy).astype(BF)
    df = (mm_t(dy, shrink) * slope.astype(F32)).astype(BF)
    grad_fbias = jnp.sum(df.astype(F32), axis=0)
    grad_expand = t_mm(n, df).astype(BF)
    df, grad_shrink, grad_expand = lax.optimization_barrier((df, grad_shrink, grad_expand))
    ffn = send((grad_expand, grad_shrink))
    dn = mm_t(df, expand)
    dm, grad_gain_two, grad_shift_two = norm_back(m, stats_two, gains[3], dn)
    dm = dm + wide
    dq_m = dm.astype(BF)
    grad_pbias = jnp.sum(dq_m.astype(F32), axis=0)
    grad_output = t_mm(a, dq_m).astype(BF)
    da = mm_t(dq_m, output).astype(BF)
    dc, z = attend_bwd(c, da, bias)
    width = attend.shape[0]
    sums = jnp.sum(dc.astype(F32), axis=0)
    grad_attend = t_mm(u, dc).astype(BF)
    dc, grad_attend, grad_output = lax.optimization_barrier((dc, grad_attend, grad_output))
    att = send((grad_attend, grad_output))
    du = mm_t(dc, attend)
    g, grad_gain_one, grad_shift_one = norm_back(s.astype(F32), stats_one, gains[0], du)
    g = (g + dm).astype(BF)
    grad_vectors = jnp.stack(
        [grad_gain_one, grad_shift_one, grad_pbias, grad_gain_two, grad_shift_two, grad_last]
    )
    grad_biases = jnp.concatenate([sums[:width], sums[2 * width :], grad_fbias])
    return g, (att, ffn), (z, grad_vectors, grad_biases)


class Sender:
    def __init__(self):
        self.last = None

    def __call__(self, grads):
        owned = tuple(
            lax.psum_scatter(g, "shard", scatter_dimension=0, tiled=True) for g in grads
        )
        if self.last is not None:
            owned, self.last = lax.optimization_barrier((owned, self.last))
        self.last = lax.psum(owned, "rep")
        return self.last


def adam(weight, moment, square, grad, rate, decay):
    moment_new = 0.9 * moment + 0.1 * grad
    square_new = 0.999 * square + 0.001 * grad * grad
    first_hat = moment_new / (1.0 - 0.9**STEP)
    second_hat = square_new / (1.0 - 0.999**STEP)
    weight_new = weight - rate * (first_hat / (jnp.sqrt(second_hat) + 1e-08) + decay * weight)
    return (moment_new, square_new, weight_new)


def shards(
    images,
    cotangent,
    window_map,
    shift_mask,
    rel_index,
    attend_weight,
    attend_moment,
    attend_square,
    output_weight,
    output_moment,
    output_square,
    expand_weight,
    expand_moment,
    expand_square,
    reduce_weight,
    reduce_moment,
    reduce_square,
    bias_table,
    table_moment,
    table_square,
    layer_vectors,
    vector_moment,
    vector_square,
    wide_bias,
    biases_moment,
    biases_square,
):
    layers = attend_weight.shape[0]
    windows = shift_mask.shape[0]
    count, tokens, width = images.shape
    ranks = lax.axis_size("shard")

    small = jnp.concatenate(
        [item.astype(BF).reshape(-1) for item in (layer_vectors, wide_bias, bias_table)]
    )
    small = lax.all_gather(small, "shard", axis=0)
    cut_one = layer_vectors.size
    cut_two = cut_one + wide_bias.size
    vectors = small[:, :cut_one].reshape((ranks,) + layer_vectors.shape)
    vectors = vectors.transpose(1, 2, 0, 3).reshape(layers, 6, width).astype(F32)
    biases = small[:, cut_one:cut_two].reshape((ranks,) + wide_bias.shape)
    biases = biases.transpose(1, 0, 2).reshape(layers, -1).astype(F32)
    table = small[:, cut_two:].reshape((ranks,) + bias_table.shape)
    table = table.transpose(1, 0, 2, 3).reshape(layers, -1, bias_table.shape[2])

    weights = []
    for layer in range(layers):
        mats = tuple(
            lax.all_gather(item[layer].astype(BF), "shard", axis=0, tiled=True)
            for item in (attend_weight, output_weight, expand_weight, reduce_weight)
        )
        weights.append(mats + (vectors[layer], biases[layer]))

    mask_term = -100.0 * shift_mask.astype(F32)
    onehot = relative_table(rel_index, table.shape[2])
    bias = [
        pair_bias(table[layer], onehot, mask_term * float(layer % 2)) for layer in range(layers)
    ]
    orders = [padded_order(window_map[layer], windows) for layer in range(layers)]
    slots = orders[0].shape[0]
    token_ids = jnp.arange(tokens, dtype=jnp.int32)
    to_slots = [(o[:, None] == token_ids[None, :]).astype(BF) for o in orders]
    moves = [
        ((orders[l + 1][:, None] == orders[l][None, :]) & (orders[l + 1][:, None] >= 0)).astype(BF)
        for l in range(layers - 1)
    ]

    flat = lambda x: x.astype(BF).reshape(count * slots, width)
    split = lambda x: x.reshape(count, slots, width)
    state = flat(place(to_slots[0], images, 1))
    saved_all = []
    for layer in range(layers):
        out, saved = forward_layer(state, bias[layer], weights[layer])
        saved_all.append(saved)
        if layer + 1 < layers:
            state = flat(place(moves[layer], split(out), 1))
    block_out = place(to_slots[-1], split(out), 0).astype(BF)

    send = Sender()
    g = flat(place(to_slots[-1], cotangent, 1))
    sent = [None] * layers
    little = [None] * layers
    for layer in reversed(range(layers)):
        g, sent[layer], little[layer] = backward_layer(
            g, bias[layer], weights[layer], saved_all[layer], send
        )
        if layer > 0:
            g = flat(place(moves[layer - 1], split(g), 0))
    grad_state = place(to_slots[0], split(g), 0)

    size = rel_index.shape[0]
    z = jnp.stack([item[0] for item in little]).reshape(layers, -1, ROWS, LANES)
    z = z[:, :, :size, :size] + z[:, :, size : 2 * size, size : 2 * size]
    g_table = jnp.einsum("lhij,ijr->lhr", z, onehot, precision=lax.Precision.HIGHEST)
    g_vectors = jnp.stack([item[1] for item in little])
    g_biases = jnp.stack([item[2] for item in little])
    g_small = jnp.concatenate(
        [
            g_vectors.reshape(layers, 6, ranks, -1).transpose(2, 0, 1, 3).reshape(ranks, -1),
            g_biases.reshape(layers, ranks, -1).transpose(1, 0, 2).reshape(ranks, -1),
            g_table.reshape(layers, ranks, -1).transpose(1, 0, 2).reshape(ranks, -1),
        ],
        axis=1,
    )
    g_small = lax.psum(g_small, ("rep", "shard"))
    g_small = lax.dynamic_index_in_dim(g_small, lax.axis_index("shard"), 0, keepdims=False)
    own = lambda index, which: jnp.stack([sent[l][index][which] for l in range(layers)]).astype(F32)
    stacked = (
        own(0, 0),
        own(0, 1),
        own(1, 0),
        own(1, 1),
        g_small[cut_two:].reshape(bias_table.shape),
        g_small[:cut_one].reshape(layer_vectors.shape),
        g_small[cut_one:cut_two].reshape(wide_bias.shape),
    )
    ma, sa, wa = adam(
        attend_weight, attend_moment, attend_square, stacked[0], 3.0 * D ** (-0.5), 0.05
    )
    mo, so, wo = adam(
        output_weight, output_moment, output_square, stacked[1], 3.0 * (8.0 / D) ** 0.5, 0.05
    )
    me, se, we = adam(
        expand_weight, expand_moment, expand_square, stacked[2], 3.0 * D ** (-0.5), 0.05
    )
    mr, sr, wr = adam(
        reduce_weight, reduce_moment, reduce_square, stacked[3], 3.0 * FF ** (-0.5), 0.05
    )
    mt, st, wt = adam(bias_table, table_moment, table_square, stacked[4], 3.0, 0.0)
    mv, sv, wv = adam(layer_vectors, vector_moment, vector_square, stacked[5], 1.0, 0.0)
    mb, sb, wb = adam(wide_bias, biases_moment, biases_square, stacked[6], 1.5, 0.0)
    return (
        block_out,
        grad_state,
        ma,
        sa,
        wa,
        mo,
        so,
        wo,
        me,
        se,
        we,
        mr,
        sr,
        wr,
        mt,
        st,
        wt,
        mv,
        sv,
        wv,
        mb,
        sb,
        wb,
    )


def solution(mesh):
    return jax.shard_map(
        shards,
        mesh=mesh,
        in_specs=(
            P(("rep", "shard"), None, None),
            P(("rep", "shard"), None, None),
            P(),
            P(),
            P(),
            P(None, "shard", None),
            P(None, "shard", None),
            P(None, "shard", None),
            P(None, "shard", None),
            P(None, "shard", None),
            P(None, "shard", None),
            P(None, "shard", None),
            P(None, "shard", None),
            P(None, "shard", None),
            P(None, "shard", None),
            P(None, "shard", None),
            P(None, "shard", None),
            P(None, "shard", None),
            P(None, "shard", None),
            P(None, "shard", None),
            P(None, None, "shard"),
            P(None, None, "shard"),
            P(None, None, "shard"),
            P(None, "shard"),
            P(None, "shard"),
            P(None, "shard"),
        ),
        out_specs=(
            P(("rep", "shard"), None, None),
            P(("rep", "shard"), None, None),
            P(None, "shard", None),
            P(None, "shard", None),
            P(None, "shard", None),
            P(None, "shard", None),
            P(None, "shard", None),
            P(None, "shard", None),
            P(None, "shard", None),
            P(None, "shard", None),
            P(None, "shard", None),
            P(None, "shard", None),
            P(None, "shard", None),
            P(None, "shard", None),
            P(None, "shard", None),
            P(None, "shard", None),
            P(None, "shard", None),
            P(None, None, "shard"),
            P(None, None, "shard"),
            P(None, None, "shard"),
            P(None, "shard"),
            P(None, "shard"),
            P(None, "shard"),
        ),
        check_vma=False,
    )
```

```python
import jax
import jax.numpy as jnp
from jax import lax
from jax.experimental import pallas as pl
from jax.experimental.pallas import tpu as pltpu
from jax.sharding import PartitionSpec as P

D = 512
FF = 2048
STEP = 10
DEPTH = 32
LANES = 128
PACK = LANES // DEPTH
ROWS = 112
SCALE = DEPTH ** (-0.5)
BF = jnp.bfloat16
F32 = jnp.float32


def dot(left, right, dims):
    return lax.dot_general(left, right, (dims, ((), ())), preferred_element_type=F32)


def mm(left, right):
    return dot(left, right, ((1,), (0,)))


def mm_t(left, right):
    return dot(left, right, ((1,), (1,)))


def t_mm(left, right):
    return dot(left, right, ((0,), (0,)))


def head_masks():
    lane = lax.broadcasted_iota(jnp.int32, (1, LANES), 1)
    return [(lane // DEPTH == h) for h in range(PACK)]


def stack_heads(x, masks):
    return jnp.concatenate([x * m.astype(F32).astype(BF) for m in masks], axis=0)


def pad_keys(x):
    return jnp.concatenate([x, jnp.zeros((LANES - ROWS, LANES), x.dtype)], axis=0)


def pick_heads(x, masks):
    out = x[0:ROWS]
    for h in range(1, PACK):
        out = jnp.where(masks[h], x[h * ROWS : (h + 1) * ROWS], out)
    return out


def softmax_rows(s):
    e = jnp.exp(s - jnp.max(s, axis=-1, keepdims=True))
    return e * (1.0 / jnp.sum(e, axis=-1, keepdims=True))


def attend_fwd_kernel(c_ref, bias_ref, a_ref):
    masks = head_masks()
    width = a_ref.shape[1]
    for g in range(width // LANES):
        col = g * LANES
        q = c_ref[:, col : col + LANES]
        k = pad_keys(c_ref[:, width + col : width + col + LANES])
        v = pad_keys(c_ref[:, 2 * width + col : 2 * width + col + LANES])
        s = mm_t(stack_heads(q, masks), k) * SCALE
        s = s + bias_ref[0, g * PACK * ROWS : (g + 1) * PACK * ROWS, :]
        p = softmax_rows(s).astype(BF)
        a_ref[:, col : col + LANES] = pick_heads(mm(p, v), masks).astype(BF)


def attend_bwd_kernel(c_ref, da_ref, bias_ref, dc_ref, z_ref):
    masks = head_masks()
    width = da_ref.shape[1]

    @pl.when((pl.program_id(0) == 0) & (pl.program_id(1) == 0))
    def _():
        z_ref[...] = jnp.zeros_like(z_ref)

    for g in range(width // LANES):
        col = g * LANES
        rows = slice(g * PACK * ROWS, (g + 1) * PACK * ROWS)
        q = c_ref[:, col : col + LANES]
        k = pad_keys(c_ref[:, width + col : width + col + LANES])
        v = pad_keys(c_ref[:, 2 * width + col : 2 * width + col + LANES])
        qs = stack_heads(q, masks)
        ds = stack_heads(da_ref[:, col : col + LANES], masks)
        p = softmax_rows(mm_t(qs, k) * SCALE + bias_ref[0, rows, :])
        dp = mm_t(ds, v)
        inner = jnp.sum(p * dp, axis=-1, keepdims=True)
        dz = (p * (dp - inner)).astype(BF)
        z_ref[rows, :] += dz.astype(F32)
        dv = t_mm(p.astype(BF), ds)
        dk = t_mm(dz, qs) * SCALE
        dq = pick_heads(mm(dz, k), masks) * SCALE
        dc_ref[:, col : col + LANES] = dq.astype(BF)
        dc_ref[:, width + col : width + col + LANES] = dk[:ROWS].astype(BF)
        dc_ref[:, 2 * width + col : 2 * width + col + LANES] = dv[:ROWS].astype(BF)


def attend_fwd(c, bias):
    pairs, stacked, _ = bias.shape
    images = c.shape[0] // (pairs * ROWS)
    width = c.shape[1] // 3
    row = lambda t, b: (b * pairs + t, 0)
    return pl.pallas_call(
        attend_fwd_kernel,
        grid=(pairs, images),
        in_specs=[
            pl.BlockSpec((ROWS, 3 * width), row),
            pl.BlockSpec((1, stacked, LANES), lambda t, b: (t, 0, 0)),
        ],
        out_specs=pl.BlockSpec((ROWS, width), row),
        out_shape=jax.ShapeDtypeStruct((c.shape[0], width), BF),
        compiler_params=pltpu.CompilerParams(vmem_limit_bytes=32 * 1024 * 1024),
        cost_estimate=pl.CostEstimate(
            flops=4 * pairs * images * stacked * LANES * LANES,
            bytes_accessed=c.size * 3 + bias.size * 4,
            transcendentals=pairs * images * stacked * LANES,
        ),
    )(c, bias)


def attend_bwd(c, da, bias):
    pairs, stacked, _ = bias.shape
    images = c.shape[0] // (pairs * ROWS)
    width = c.shape[1] // 3
    row = lambda t, b: (b * pairs + t, 0)
    return pl.pallas_call(
        attend_bwd_kernel,
        grid=(pairs, images),
        in_specs=[
            pl.BlockSpec((ROWS, 3 * width), row),
            pl.BlockSpec((ROWS, width), row),
            pl.BlockSpec((1, stacked, LANES), lambda t, b: (t, 0, 0)),
        ],
        out_specs=[
            pl.BlockSpec((ROWS, 3 * width), row),
            pl.BlockSpec((stacked, LANES), lambda t, b: (0, 0)),
        ],
        out_shape=[
            jax.ShapeDtypeStruct(c.shape, BF),
            jax.ShapeDtypeStruct((stacked, LANES), F32),
        ],
        compiler_params=pltpu.CompilerParams(vmem_limit_bytes=32 * 1024 * 1024),
        cost_estimate=pl.CostEstimate(
            flops=10 * pairs * images * stacked * LANES * LANES,
            bytes_accessed=c.size * 5 + bias.size * 4,
            transcendentals=pairs * images * stacked * LANES,
        ),
    )(c, da, bias)


def row_stats(v):
    mean = jnp.mean(v, axis=-1, keepdims=True)
    centered = v - mean
    rstd = lax.rsqrt(jnp.mean(centered * centered, axis=-1, keepdims=True) + 1e-05)
    return mean, rstd


def norm_rows(v, gain, shift):
    mean, rstd = row_stats(v)
    return ((v - mean) * rstd * gain + shift).astype(BF), (mean, rstd)


def norm_back(v, stats, gain, do):
    mean, rstd = stats
    r = (v - mean) * rstd
    dg = do * gain
    grad = (
        dg - jnp.mean(dg, axis=-1, keepdims=True) - r * jnp.mean(dg * r, axis=-1, keepdims=True)
    ) * rstd
    return grad, jnp.sum(do * r, axis=0), jnp.sum(do, axis=0)


def gelu_both(f):
    cdf = 0.5 * (1.0 + lax.erf(f * 0.7071067811865476))
    slope = cdf + f * jnp.exp(-0.5 * f * f) * 0.3989422804014327
    return (f * cdf).astype(BF), slope.astype(BF)


def relative_table(rel_index, rows):
    return (rel_index[:, :, None] == jnp.arange(rows, dtype=jnp.int32)[None, None, :]).astype(F32)


def pair_bias(table, onehot, penalty):
    position = jnp.einsum("hr,ijr->hij", table.astype(F32), onehot, precision=lax.Precision.HIGHEST)
    size = position.shape[-1]
    both = position[None, None] + penalty.reshape(-1, 2, 1, size, size)
    first = jnp.pad(
        both[:, 0], ((0, 0), (0, 0), (0, ROWS - size), (0, LANES - size)), constant_values=-1e30
    )
    second = jnp.pad(
        both[:, 1],
        ((0, 0), (0, 0), (size, ROWS - 2 * size), (size, LANES - 2 * size)),
        constant_values=-1e30,
    )
    row = lax.broadcasted_iota(jnp.int32, (ROWS, LANES), 0)
    lane = lax.broadcasted_iota(jnp.int32, (ROWS, LANES), 1)
    both = jnp.maximum(first, second)
    both = jnp.where((row >= 2 * size) & (lane < size), 0.0, both)
    return both.reshape(penalty.shape[0] // 2, -1, LANES)


def padded_order(order, windows):
    pairs = order.reshape(windows // 2, -1)
    return jnp.pad(pairs, ((0, 0), (0, ROWS - pairs.shape[1])), constant_values=-1).reshape(-1)


def place(onehot, x, contract):
    count = x.shape[0]
    hot = jnp.broadcast_to(onehot[None], (count,) + onehot.shape)
    return lax.dot_general(
        hot, x, (((contract + 1,), (1,)), ((0,), (0,))), preferred_element_type=F32
    )


def forward_layer(s, bias, weights):
    attend, output, expand, shrink, gains, offsets = weights
    width = attend.shape[0]
    qkv_bias = jnp.concatenate(
        [offsets[:width], jnp.zeros((width,), F32), offsets[width : 2 * width]]
    )
    wide = s.astype(F32)
    u, stats_one = norm_rows(wide, gains[0], gains[1])
    c = (mm(u, attend) + qkv_bias).astype(BF)
    a = attend_fwd(c, bias)
    m = wide + mm(a, output) + gains[2]
    n, stats_two = norm_rows(m, gains[3], gains[4])
    e, slope = gelu_both(mm(n, expand) + offsets[2 * width :])
    out = (m + mm(e, shrink) + gains[5]).astype(BF)
    return out, (s, u, stats_one, c, a, m, n, stats_two, e, slope)


def backward_layer(gs, bias, weights, saved, send):
    attend, output, expand, shrink, gains, offsets = weights
    s, u, stats_one, c, a, m, n, stats_two, e, slope = saved
    dy = gs.astype(BF)
    wide = gs.astype(F32)
    grad_last = jnp.sum(dy.astype(F32), axis=0)
    grad_shrink = t_mm(e, dy).astype(BF)
    df = (mm_t(dy, shrink) * slope.astype(F32)).astype(BF)
    grad_fbias = jnp.sum(df.astype(F32), axis=0)
    grad_expand = t_mm(n, df).astype(BF)
    df, grad_shrink, grad_expand = lax.optimization_barrier((df, grad_shrink, grad_expand))
    ffn = send((grad_expand, grad_shrink))
    dn = mm_t(df, expand)
    dm, grad_gain_two, grad_shift_two = norm_back(m, stats_two, gains[3], dn)
    dm = dm + wide
    dq_m = dm.astype(BF)
    grad_pbias = jnp.sum(dq_m.astype(F32), axis=0)
    grad_output = t_mm(a, dq_m).astype(BF)
    da = mm_t(dq_m, output).astype(BF)
    dc, z = attend_bwd(c, da, bias)
    width = attend.shape[0]
    sums = jnp.sum(dc.astype(F32), axis=0)
    grad_attend = t_mm(u, dc).astype(BF)
    dc, grad_attend, grad_output = lax.optimization_barrier((dc, grad_attend, grad_output))
    att = send((grad_attend, grad_output))
    du = mm_t(dc, attend)
    g, grad_gain_one, grad_shift_one = norm_back(s.astype(F32), stats_one, gains[0], du)
    g = (g + dm).astype(BF)
    grad_vectors = jnp.stack(
        [grad_gain_one, grad_shift_one, grad_pbias, grad_gain_two, grad_shift_two, grad_last]
    )
    grad_biases = jnp.concatenate([sums[:width], sums[2 * width :], grad_fbias])
    return g, (att, ffn), (z, grad_vectors, grad_biases)


def scatter_grads(grads):
    return tuple(lax.psum_scatter(g, "shard", scatter_dimension=0, tiled=True) for g in grads)


def adam(weight, moment, square, grad, rate, decay):
    moment_new = 0.9 * moment + 0.1 * grad
    square_new = 0.999 * square + 0.001 * grad * grad
    first_hat = moment_new / (1.0 - 0.9**STEP)
    second_hat = square_new / (1.0 - 0.999**STEP)
    weight_new = weight - rate * (first_hat / (jnp.sqrt(second_hat) + 1e-08) + decay * weight)
    return (moment_new, square_new, weight_new)


def shards(
    images,
    cotangent,
    window_map,
    shift_mask,
    rel_index,
    attend_weight,
    attend_moment,
    attend_square,
    output_weight,
    output_moment,
    output_square,
    expand_weight,
    expand_moment,
    expand_square,
    reduce_weight,
    reduce_moment,
    reduce_square,
    bias_table,
    table_moment,
    table_square,
    layer_vectors,
    vector_moment,
    vector_square,
    wide_bias,
    biases_moment,
    biases_square,
):
    layers = attend_weight.shape[0]
    windows = shift_mask.shape[0]
    count, tokens, width = images.shape
    ranks = lax.axis_size("shard")

    small = jnp.concatenate(
        [item.astype(BF).reshape(-1) for item in (layer_vectors, wide_bias, bias_table)]
    )
    small = lax.all_gather(small, "shard", axis=0)
    cut_one = layer_vectors.size
    cut_two = cut_one + wide_bias.size
    vectors = small[:, :cut_one].reshape((ranks,) + layer_vectors.shape)
    vectors = vectors.transpose(1, 2, 0, 3).reshape(layers, 6, width).astype(F32)
    biases = small[:, cut_one:cut_two].reshape((ranks,) + wide_bias.shape)
    biases = biases.transpose(1, 0, 2).reshape(layers, -1).astype(F32)
    table = small[:, cut_two:].reshape((ranks,) + bias_table.shape)
    table = table.transpose(1, 0, 2, 3).reshape(layers, -1, bias_table.shape[2])

    weights = []
    for layer in range(layers):
        mats = tuple(
            lax.all_gather(item[layer].astype(BF), "shard", axis=0, tiled=True)
            for item in (attend_weight, output_weight, expand_weight, reduce_weight)
        )
        weights.append(mats + (vectors[layer], biases[layer]))

    mask_term = -100.0 * shift_mask.astype(F32)
    onehot = relative_table(rel_index, table.shape[2])
    bias = [
        pair_bias(table[layer], onehot, mask_term * float(layer % 2)) for layer in range(layers)
    ]
    orders = [padded_order(window_map[layer], windows) for layer in range(layers)]
    slots = orders[0].shape[0]
    token_ids = jnp.arange(tokens, dtype=jnp.int32)
    to_slots = [(o[:, None] == token_ids[None, :]).astype(BF) for o in orders]
    moves = [
        ((orders[l + 1][:, None] == orders[l][None, :]) & (orders[l + 1][:, None] >= 0)).astype(BF)
        for l in range(layers - 1)
    ]

    flat = lambda x: x.astype(BF).reshape(count * slots, width)
    split = lambda x: x.reshape(count, slots, width)
    state = flat(place(to_slots[0], images, 1))
    saved_all = []
    for layer in range(layers):
        out, saved = forward_layer(state, bias[layer], weights[layer])
        saved_all.append(saved)
        if layer + 1 < layers:
            state = flat(place(moves[layer], split(out), 1))
    block_out = place(to_slots[-1], split(out), 0).astype(BF)

    send = scatter_grads
    g = flat(place(to_slots[-1], cotangent, 1))
    sent = [None] * layers
    little = [None] * layers
    for layer in reversed(range(layers)):
        g, sent[layer], little[layer] = backward_layer(
            g, bias[layer], weights[layer], saved_all[layer], send
        )
        if layer > 0:
            g = flat(place(moves[layer - 1], split(g), 0))
    grad_state = place(to_slots[0], split(g), 0)

    size = rel_index.shape[0]
    z = jnp.stack([item[0] for item in little]).reshape(layers, -1, ROWS, LANES)
    z = z[:, :, :size, :size] + z[:, :, size : 2 * size, size : 2 * size]
    g_table = jnp.einsum("lhij,ijr->lhr", z, onehot, precision=lax.Precision.HIGHEST)
    g_vectors = jnp.stack([item[1] for item in little])
    g_biases = jnp.stack([item[2] for item in little])
    g_small = jnp.concatenate(
        [
            g_vectors.reshape(layers, 6, ranks, -1).transpose(2, 0, 1, 3).reshape(ranks, -1),
            g_biases.reshape(layers, ranks, -1).transpose(1, 0, 2).reshape(ranks, -1),
            g_table.reshape(layers, ranks, -1).transpose(1, 0, 2).reshape(ranks, -1),
        ],
        axis=1,
    )
    g_small = lax.psum(g_small.astype(BF), "shard")
    g_small = lax.dynamic_index_in_dim(g_small, lax.axis_index("shard"), 0, keepdims=False)
    sent = lax.psum(sent, "rep")
    g_small = lax.psum(g_small, "rep").astype(F32)
    own = lambda index, which: jnp.stack([sent[l][index][which] for l in range(layers)]).astype(F32)
    stacked = (
        own(0, 0),
        own(0, 1),
        own(1, 0),
        own(1, 1),
        g_small[cut_two:].reshape(bias_table.shape),
        g_small[:cut_one].reshape(layer_vectors.shape),
        g_small[cut_one:cut_two].reshape(wide_bias.shape),
    )
    ma, sa, wa = adam(
        attend_weight, attend_moment, attend_square, stacked[0], 3.0 * D ** (-0.5), 0.05
    )
    mo, so, wo = adam(
        output_weight, output_moment, output_square, stacked[1], 3.0 * (8.0 / D) ** 0.5, 0.05
    )
    me, se, we = adam(
        expand_weight, expand_moment, expand_square, stacked[2], 3.0 * D ** (-0.5), 0.05
    )
    mr, sr, wr = adam(
        reduce_weight, reduce_moment, reduce_square, stacked[3], 3.0 * FF ** (-0.5), 0.05
    )
    mt, st, wt = adam(bias_table, table_moment, table_square, stacked[4], 3.0, 0.0)
    mv, sv, wv = adam(layer_vectors, vector_moment, vector_square, stacked[5], 1.0, 0.0)
    mb, sb, wb = adam(wide_bias, biases_moment, biases_square, stacked[6], 1.5, 0.0)
    return (
        block_out,
        grad_state,
        ma,
        sa,
        wa,
        mo,
        so,
        wo,
        me,
        se,
        we,
        mr,
        sr,
        wr,
        mt,
        st,
        wt,
        mv,
        sv,
        wv,
        mb,
        sb,
        wb,
    )


def solution(mesh):
    return jax.shard_map(
        shards,
        mesh=mesh,
        in_specs=(
            P(("rep", "shard"), None, None),
            P(("rep", "shard"), None, None),
            P(),
            P(),
            P(),
            P(None, "shard", None),
            P(None, "shard", None),
            P(None, "shard", None),
            P(None, "shard", None),
            P(None, "shard", None),
            P(None, "shard", None),
            P(None, "shard", None),
            P(None, "shard", None),
            P(None, "shard", None),
            P(None, "shard", None),
            P(None, "shard", None),
            P(None, "shard", None),
            P(None, "shard", None),
            P(None, "shard", None),
            P(None, "shard", None),
            P(None, None, "shard"),
            P(None, None, "shard"),
            P(None, None, "shard"),
            P(None, "shard"),
            P(None, "shard"),
            P(None, "shard"),
        ),
        out_specs=(
            P(("rep", "shard"), None, None),
            P(("rep", "shard"), None, None),
            P(None, "shard", None),
            P(None, "shard", None),
            P(None, "shard", None),
            P(None, "shard", None),
            P(None, "shard", None),
            P(None, "shard", None),
            P(None, "shard", None),
            P(None, "shard", None),
            P(None, "shard", None),
            P(None, "shard", None),
            P(None, "shard", None),
            P(None, "shard", None),
            P(None, "shard", None),
            P(None, "shard", None),
            P(None, "shard", None),
            P(None, None, "shard"),
            P(None, None, "shard"),
            P(None, None, "shard"),
            P(None, "shard"),
            P(None, "shard"),
            P(None, "shard"),
        ),
        check_vma=False,
    )
```
